32 devices in a mesh: block: 4 (over x, core), tok: 8 (over z, y).
Axes of the slice: x: 2, y: 2, z: 4, core: 2. Of those that a mesh axis runs over, the one named last changes fastest.
Arguments:
- query: bfloat16 [12288, 10, 256], P(('block', 'tok')), may hold values from -6 to 6
- key: bfloat16 [12288, 10, 256], P(('block', 'tok')), may hold values from -6 to 6
- value: bfloat16 [12288, 10, 256], P(('block', 'tok')), may hold values from -6 to 6
- rates: float32 [10, 12288], P(None, ('block', 'tok')), may hold values from 0.01 to 0.3
- init_weights: float32 [10, 3, 256, 256], P(None, None, 'tok'), may hold values from -0.375 to 0.375
Outputs:
- output: bfloat16 [12288, 10, 256], P(('block', 'tok'))
- states: float32 [4, 10, 3, 256, 256], P('block', None, None, 'tok')
The draws below stay inside these ranges and needn't reach their ends.
All inputs are finite; a program needn't handle non-finite values.
Results may differ from the reference program's by a relative error of at most 0.013.
The reference program's roundings to bfloat16 on the way count: a program that leaves them out, or rounds other values in their place, can miss the bound.
Values may be sent and summed in bfloat16 or wider, within the bound.
A program may use at most 64 MiB of HBM per device.

```python
import math
import jax
import jax.numpy as jnp
from jax import lax

DH = 256
HID = 256
HEADS = 10
BLOCK = 3072
BLOCKS = 4
TOKENS = 12288


def block_levels(stream_key, shape, split, smallest, high):
    loudness = 1.0
    for position, shards_of in split:
        steps = jax.random.uniform(jax.random.fold_in(jax.random.fold_in(stream_key, 6), position), (shards_of,), jnp.float32, smallest / len(split), high / len(split))
        loudness = loudness * jnp.repeat(jnp.exp(steps), shape[position] // shards_of).reshape((-1,) + (1,) * (len(shape) - 1 - position))
    return loudness


def normal_values(stream_key, dims, spread, most, pieces=(), kind=jnp.bfloat16):
    result = spread * jax.random.normal(stream_key, dims, jnp.float32)
    if pieces:
        result = result * block_levels(stream_key, dims, pieces, -0.22, 0.18)
    return jnp.clip(result, -most, most).astype(kind)


def setup_inputs(seed: int = 0) -> dict:
    key_of = jax.random.split(jax.random.key(seed), 6)
    query = normal_values(key_of[0], (TOKENS, HEADS, DH), 1.0, 6.0, ((0, 32),))
    key = normal_values(key_of[1], (TOKENS, HEADS, DH), 1.0, 6.0, ((0, 32),))
    value = normal_values(key_of[2], (TOKENS, HEADS, DH), 1.0, 6.0, ((0, 32),))
    rates = jnp.clip(jnp.exp(math.log(0.3) - 3.4011974 * jax.random.uniform(key_of[3], (HEADS, TOKENS), jnp.float32) ** block_levels(key_of[3], (HEADS, TOKENS), ((1, 32),), -0.2, 0.2)), 0.01, 0.3)
    init_weights = normal_values(key_of[4], (HEADS, 3, HID, DH), DH ** -0.5, 0.375, ((2, 8),), jnp.float32)
    return {"query": query, "key": key, "value": value, "rates": rates, "init_weights": init_weights}


def block_step(weights, inputs):
    quer, keys, vals, lrs = inputs
    wb = weights.astype(jnp.bfloat16)

    def forward(rows_in):
        a_val = jnp.dot(rows_in, wb[0].T, preferred_element_type=jnp.float32)
        b_val = jnp.dot(rows_in, wb[1].T, preferred_element_type=jnp.float32)
        sig = jax.nn.sigmoid(a_val)
        s_val = a_val * sig
        return (a_val, b_val, sig, s_val, (s_val * b_val).astype(jnp.bfloat16))
    _, _, _, _, hid_q = forward(quer)
    out_rows = jnp.dot(hid_q, wb[2], preferred_element_type=jnp.float32).astype(jnp.bfloat16)
    a_val, b_val, sig, s_val, hid_k = forward(keys)
    factor = lrs * (1.0 / math.sqrt(BLOCK))
    g_val = (-(factor[:, None] * vals.astype(jnp.float32))).astype(jnp.bfloat16)
    dhid = jnp.dot(g_val, wb[2].T, preferred_element_type=jnp.float32)
    dsil = sig * (1.0 + a_val * (1.0 - sig))
    d_a = (dhid * b_val * dsil).astype(jnp.bfloat16)
    d_b = (dhid * s_val).astype(jnp.bfloat16)
    grads = jnp.stack([jnp.dot(d_a.T, keys, preferred_element_type=jnp.float32), jnp.dot(d_b.T, keys, preferred_element_type=jnp.float32), jnp.dot(hid_k.T, g_val, preferred_element_type=jnp.float32)], axis=0)
    upd = weights - grads
    ratio = jnp.sqrt((lax.optimization_barrier(jnp.mean(weights * weights, axis=-1)) + 1e-06) / (lax.optimization_barrier(jnp.mean(upd * upd, axis=-1)) + 1e-06))
    new_w = upd * ratio[..., None]
    return (new_w, (out_rows, new_w))

def reference(query, key, value, rates, init_weights):
    outs = []
    saved = []
    for head in range(HEADS):
        xs = (query[:, head, :].reshape(BLOCKS, BLOCK, DH), key[:, head, :].reshape(BLOCKS, BLOCK, DH), value[:, head, :].reshape(BLOCKS, BLOCK, DH), rates[head].reshape(BLOCKS, BLOCK))
        _, (out_rows, news) = lax.scan(block_step, init_weights[head], xs)
        outs.append(out_rows.reshape(TOKENS, DH))
        saved.append(news)
    return (jnp.stack(outs, axis=1), jnp.stack(saved, axis=1))
```

```python
import functools
import math

import jax
import jax.numpy as jnp
from jax import lax
from jax.experimental import pallas as pl
from jax.experimental.pallas import tpu as pltpu
from jax.sharding import PartitionSpec as P

MESH = pl.DeviceIdType.MESH
PAIR = 2


def nt(left, right):
    return lax.dot_general(
        left, right, (((1,), (1,)), ((), ())), preferred_element_type=jnp.float32
    )


def nn(left, right):
    return lax.dot_general(
        left, right, (((1,), (0,)), ((), ())), preferred_element_type=jnp.float32
    )


def sigmoid(x):
    return 0.5 * jnp.tanh(0.5 * x) + 0.5


def kernel(
    heads, blocks, outer,
    q_ref, k_ref, g_ref, init_ref,
    out_ref, states_ref,
    wfull, iw, sw, wn, gf, gsum, sy, gy, sz, gz,
    wi_send, wz_send, wz_recv, wy_send, wy_recv, wn_send, wn_recv,
    gy_send, gy_recv, gz_send, gz_recv,
):
    b = lax.axis_index("block")
    t = lax.axis_index("tok")
    z, y = t // PAIR, t % PAIR
    rows = init_ref.shape[2]
    half = outer * rows
    mine = pl.ds(pl.multiple_of(y * half + z * rows, rows), rows)
    my_half = pl.ds(pl.multiple_of(y * half, half), half)
    its_half = pl.ds(pl.multiple_of((1 - y) * half, half), half)
    last = blocks - 1
    peer = (b, z * PAIR + (1 - y))

    def zid(d):
        return lax.rem(z + d, outer)

    def copy(src, dst, send, recv, dev):
        return pltpu.make_async_remote_copy(
            src_ref=src, dst_ref=dst, send_sem=send, recv_sem=recv,
            device_id=dev, device_id_type=MESH,
        )

    def init_copy(h, d):
        return copy(iw.at[h], wfull.at[h, :, mine, :], wi_send.at[h, d], wz_recv.at[h, z],
                    (b, zid(d) * PAIR + y))

    def next_copy(h, d):
        return copy(sw.at[h], wfull.at[h, :, mine, :], wz_send.at[h, d], wz_recv.at[h, z],
                    (lax.rem(b + 1, blocks), zid(d) * PAIR + y))

    def wz_arrival(h, d):
        start = pl.multiple_of(y * half + zid(d) * rows, rows)
        return copy(sw.at[h], wfull.at[h, :, pl.ds(start, rows), :], wz_send.at[h, d],
                    wz_recv.at[h, zid(d)], peer)

    def pass_copy(h):
        return copy(states_ref.at[h], wn.at[h], wn_send.at[h], wn_recv.at[h],
                    (lax.rem(b + 1, blocks), t))

    def fwd_copy(h):
        view = wfull.at[h, :, my_half, :]
        return copy(view, view, wy_send.at[h], wy_recv.at[h], peer)

    def fwd_arrival(h):
        view = wfull.at[h, :, its_half, :]
        return copy(view, view, wy_send.at[h], wy_recv.at[h], peer)

    def gy_copy(h, m):
        return copy(sy.at[h, m], gy.at[h, m], gy_send.at[h, m], gy_recv.at[h, m], peer)

    def gz_copy(h, d):
        part = pl.ds(pl.multiple_of(zid(d) * rows, rows), rows)
        return copy(sz.at[h, :, part, :], gz.at[h, z], gz_send.at[h, d], gz_recv.at[h, z],
                    (b, zid(d) * PAIR + y))

    def gz_arrival(h, d):
        return copy(sz.at[h, :, pl.ds(0, rows), :], gz.at[h, zid(d)], gz_send.at[h, d],
                    gz_recv.at[h, zid(d)], peer)

    barrier = pltpu.get_barrier_semaphore()

    def greet(dev):
        pl.semaphore_signal(barrier, inc=1, device_id=dev, device_id_type=MESH)

    greet(peer)
    for d in range(1, outer):
        greet((b, zid(d) * PAIR + y))

    for d in range(outer):
        greet((lax.rem(b + 1, blocks), zid(d) * PAIR + y))
        greet((lax.rem(b + last, blocks), zid(d) * PAIR + y))
    pl.semaphore_wait(barrier, 3 * outer)

    def start_init(h):
        iw[h] = init_ref[h].astype(jnp.bfloat16)
        wfull[h, :, mine, :] = iw[h]
        for d in range(1, outer):
            init_copy(h, d).start()

    def forward_weights(h):
        for d in range(1, outer):
            wz_arrival(h, d).wait_recv()

        @pl.when(b > 0)
        def _():
            wz_arrival(h, 0).wait_recv()

        fwd_copy(h).start()

    @pl.when(b == 0)
    def _():
        start_init(0)
        start_init(1)

    forward_weights(0)

    def one_head(h, _):
        fwd_arrival(h).wait_recv()
        wa, wb, wc = wfull[h, 0], wfull[h, 1], wfull[h, 2]
        keys, g = k_ref[h], g_ref[h]

        def emit(m, grad):
            gf[m] = grad
            sy[h, m] = gf[m, its_half, :].astype(jnp.bfloat16)
            gy_copy(h, m).start()

        a = nt(wa, keys)
        bb = nt(wb, keys)
        sig = sigmoid(a)
        s = a * sig
        emit(2, nn((s * bb).astype(jnp.bfloat16), g))
        dhid = nt(wc, g)
        emit(1, nn((dhid * s).astype(jnp.bfloat16), keys))
        dsil = sig * (1.0 + a * (1.0 - sig))
        emit(0, nn((dhid * bb * dsil).astype(jnp.bfloat16), keys))

        @pl.when((b == 0) & (h + 2 < heads))
        def _():
            start_init(h + 2)

        @pl.when((b == 0) & (h + 1 < heads))
        def _():
            forward_weights(h + 1)

        for m in (2, 1, 0):
            gy_copy(h, m).wait_recv()
            total = gf[m, my_half, :] + gy[h, m].astype(jnp.float32)
            gsum[m] = total
            sz[h, m] = total.astype(jnp.bfloat16)
        for d in range(1, outer):
            gz_copy(h, d).start()

        quer = q_ref[h]
        qa = nt(quer, wa)
        hid_q = (qa * sigmoid(qa) * nt(quer, wb)).astype(jnp.bfloat16)
        out_ref[h] = nn(hid_q, wc).astype(jnp.bfloat16)

        @pl.when(b == 0)
        def _():
            wn[h] = init_ref[h]

        @pl.when(b > 0)
        def _():
            pass_copy(h).wait_recv()

        current = wn[h]
        grads = gsum[:, pl.ds(pl.multiple_of(z * rows, rows), rows), :]
        for d in range(1, outer):
            gz_arrival(h, d).wait_recv()
            grads = grads + gz[h, zid(d)].astype(jnp.float32)
        upd = current - grads
        ratio = jnp.sqrt(
            (jnp.mean(current * current, axis=-1, keepdims=True) + 1e-06)
            / (jnp.mean(upd * upd, axis=-1, keepdims=True) + 1e-06)
        )
        new_w = upd * ratio
        states_ref[h] = new_w
        sw[h] = new_w.astype(jnp.bfloat16)

        @pl.when(b < last)
        def _():
            for d in range(outer):
                next_copy(h, d).start()
            pass_copy(h).start()

        @pl.when((b > 0) & (h + 1 < heads))
        def _():
            forward_weights(h + 1)

        return 0

    lax.fori_loop(0, heads, one_head, 0)

    def drain(h, _):
        @pl.when(b == 0)
        def _():
            for d in range(1, outer):
                init_copy(h, d).wait_send()

        @pl.when(b < last)
        def _():
            for d in range(outer):
                next_copy(h, d).wait_send()
            pass_copy(h).wait_send()

        fwd_copy(h).wait_send()
        for m in range(3):
            gy_copy(h, m).wait_send()
        for d in range(1, outer):
            gz_copy(h, d).wait_send()
        return 0

    lax.fori_loop(0, heads, drain, 0)


def on_device(query, key, value, rates, init_weights):
    tokens, heads, dim = query.shape
    blocks, tok = lax.axis_size("block"), lax.axis_size("tok")
    outer = tok // PAIR
    rows, hid = init_weights.shape[2], init_weights.shape[2] * tok
    half = hid // PAIR
    factor = rates * (1.0 / math.sqrt(tokens * tok))
    g = (-(factor[:, :, None] * jnp.transpose(value, (1, 0, 2)).astype(jnp.float32))).astype(jnp.bfloat16)
    q = jnp.transpose(query, (1, 0, 2))
    k = jnp.transpose(key, (1, 0, 2))
    bf16, f32 = jnp.bfloat16, jnp.float32
    dma = pltpu.SemaphoreType.DMA
    vmem = pl.BlockSpec(memory_space=pltpu.VMEM)
    out, states = pl.pallas_call(
        functools.partial(kernel, heads, blocks, outer),
        out_shape=(
            jax.ShapeDtypeStruct((heads, tokens, dim), bf16),
            jax.ShapeDtypeStruct(init_weights.shape, f32),
        ),
        in_specs=[vmem] * 4,
        out_specs=(vmem, vmem),
        scratch_shapes=[
            pltpu.VMEM((heads, 3, hid, dim), bf16),
            pltpu.VMEM((heads, 3, rows, dim), bf16),
            pltpu.VMEM((heads, 3, rows, dim), bf16),
            pltpu.VMEM((heads, 3, rows, dim), f32),
            pltpu.VMEM((3, hid, dim), f32),
            pltpu.VMEM((3, half, dim), f32),
            pltpu.VMEM((heads, 3, half, dim), bf16),
            pltpu.VMEM((heads, 3, half, dim), bf16),
            pltpu.VMEM((heads, 3, half, dim), bf16),
            pltpu.VMEM((heads, outer, 3, rows, dim), bf16),
            dma((heads, outer)), dma((heads, outer)), dma((heads, outer)),
            dma((heads,)), dma((heads,)), dma((heads,)), dma((heads,)),
            dma((heads, 3)), dma((heads, 3)),
            dma((heads, outer)), dma((heads, outer)),
        ],
        compiler_params=pltpu.CompilerParams(
            collective_id=0, has_side_effects=True, vmem_limit_bytes=48 * 1024 * 1024
        ),
        cost_estimate=pl.CostEstimate(
            flops=18 * heads * tokens * hid * dim,
            bytes_accessed=10 * heads * tokens * dim,
            transcendentals=2 * heads * tokens * hid,
        ),
    )(q, k, g, init_weights)
    return (jnp.transpose(out, (1, 0, 2)), states[None])


def solution(mesh):
    placed = (
        P(("block", "tok"), None, None),
        P(("block", "tok"), None, None),
        P(("block", "tok"), None, None),
        P(None, ("block", "tok")),
        P(None, None, "tok", None),
    )
    return jax.shard_map(
        on_device,
        mesh=mesh,
        in_specs=placed,
        out_specs=(P(("block", "tok"), None, None), P("block", None, None, "tok", None)),
        check_vma=False,
    )
```

```python
import functools
import math

import jax
import jax.numpy as jnp
from jax import lax
from jax.experimental import pallas as pl
from jax.experimental.pallas import tpu as pltpu
from jax.sharding import PartitionSpec as P

MESH = pl.DeviceIdType.MESH
LEAD = 1
DEPTH = 2
AHEAD = 3
PAIR = 2


def nt(left, right):
    return lax.dot_general(
        left, right, (((1,), (1,)), ((), ())), preferred_element_type=jnp.float32
    )


def nn(left, right):
    return lax.dot_general(
        left, right, (((1,), (0,)), ((), ())), preferred_element_type=jnp.float32
    )


def sigmoid(x):
    return 0.5 * jnp.tanh(0.5 * x) + 0.5


def kernel(
    heads, blocks, outer,
    q_ref, k_ref, g_ref, init_ref,
    out_ref, states_ref,
    wfull, iw, sw, wn, gf, gsum, sy, gy, sz, gz,
    wi_send, wz_send, wz_recv, wy_send, wy_recv, wn_send, wn_recv,
    gy_send, gy_recv, gz_send, gz_recv,
):
    b = lax.axis_index("block")
    t = lax.axis_index("tok")
    z, y = t // PAIR, t % PAIR
    rows = init_ref.shape[2]
    half = outer * rows
    mine = pl.ds(pl.multiple_of(y * half + z * rows, rows), rows)
    my_half = pl.ds(pl.multiple_of(y * half, half), half)
    its_half = pl.ds(pl.multiple_of((1 - y) * half, half), half)
    last = blocks - 1
    peer = (b, z * PAIR + (1 - y))

    def zid(d):
        return lax.rem(z + d, outer)

    def copy(src, dst, send, recv, dev):
        return pltpu.make_async_remote_copy(
            src_ref=src, dst_ref=dst, send_sem=send, recv_sem=recv,
            device_id=dev, device_id_type=MESH,
        )

    def init_copy(h, d):
        return copy(iw.at[h], wfull.at[h, :, mine, :], wi_send.at[h, d], wz_recv.at[h, z],
                    (b, zid(d) * PAIR + y))

    def next_copy(h, d):
        return copy(sw.at[h], wfull.at[h, :, mine, :], wz_send.at[h, d], wz_recv.at[h, z],
                    (lax.rem(b + 1, blocks), zid(d) * PAIR + y))

    def wz_arrival(h, d):
        start = pl.multiple_of(y * half + zid(d) * rows, rows)
        return copy(sw.at[h], wfull.at[h, :, pl.ds(start, rows), :], wz_send.at[h, d],
                    wz_recv.at[h, zid(d)], peer)

    def pass_copy(h):
        return copy(states_ref.at[h], wn.at[h], wn_send.at[h], wn_recv.at[h],
                    (lax.rem(b + 1, blocks), t))

    def fwd_copy(h):
        view = wfull.at[h, :, my_half, :]
        return copy(view, view, wy_send.at[h], wy_recv.at[h], peer)

    def fwd_arrival(h):
        view = wfull.at[h, :, its_half, :]
        return copy(view, view, wy_send.at[h], wy_recv.at[h], peer)

    def gy_copy(h, m):
        return copy(sy.at[h, m], gy.at[h, m], gy_send.at[h, m], gy_recv.at[h, m], peer)

    def gz_copy(h, d):
        part = pl.ds(pl.multiple_of(zid(d) * rows, rows), rows)
        return copy(sz.at[h, :, part, :], gz.at[h, z], gz_send.at[h, d], gz_recv.at[h, z],
                    (b, zid(d) * PAIR + y))

    def gz_arrival(h, d):
        return copy(sz.at[h, :, pl.ds(0, rows), :], gz.at[h, zid(d)], gz_send.at[h, d],
                    gz_recv.at[h, zid(d)], peer)

    barrier = pltpu.get_barrier_semaphore()

    def greet(dev):
        pl.semaphore_signal(barrier, inc=1, device_id=dev, device_id_type=MESH)

    greet(peer)
    for d in range(1, outer):
        greet((b, zid(d) * PAIR + y))

    for d in range(outer):
        greet((lax.rem(b + 1, blocks), zid(d) * PAIR + y))
        greet((lax.rem(b + last, blocks), zid(d) * PAIR + y))
    pl.semaphore_wait(barrier, 3 * outer)

    def start_init(h):
        iw[h] = init_ref[h].astype(jnp.bfloat16)
        wfull[h, :, mine, :] = iw[h]
        for d in range(1, outer):
            init_copy(h, d).start()

    def forward_weights(h):
        for d in range(1, outer):
            wz_arrival(h, d).wait_recv()

        @pl.when(b > 0)
        def _():
            wz_arrival(h, 0).wait_recv()

        fwd_copy(h).start()

    @pl.when(b == 0)
    def _():
        for h in range(min(AHEAD, heads)):
            start_init(h)

    for h in range(min(LEAD, heads)):
        forward_weights(h)

    def differentiate(h):
        fwd_arrival(h).wait_recv()
        wa, wb, wc = wfull[h, 0], wfull[h, 1], wfull[h, 2]
        keys, g = k_ref[h], g_ref[h]

        def emit(m, grad):
            gf[h, m] = grad
            sy[h, m] = gf[h, m, its_half, :].astype(jnp.bfloat16)
            gy_copy(h, m).start()

        a = nt(wa, keys)
        bb = nt(wb, keys)
        sig = sigmoid(a)
        s = a * sig
        emit(2, nn((s * bb).astype(jnp.bfloat16), g))
        dhid = nt(wc, g)
        emit(1, nn((dhid * s).astype(jnp.bfloat16), keys))
        dsil = sig * (1.0 + a * (1.0 - sig))
        emit(0, nn((dhid * bb * dsil).astype(jnp.bfloat16), keys))

    def combine(h):
        for m in (2, 1, 0):
            gy_copy(h, m).wait_recv()
            total = gf[h, m, my_half, :] + gy[h, m].astype(jnp.float32)
            gsum[h, m] = total
            sz[h, m] = total.astype(jnp.bfloat16)
        for d in range(1, outer):
            gz_copy(h, d).start()

    def answer(h):
        wa, wb, wc = wfull[h, 0], wfull[h, 1], wfull[h, 2]
        quer = q_ref[h]
        qa = nt(quer, wa)
        hid_q = (qa * sigmoid(qa) * nt(quer, wb)).astype(jnp.bfloat16)
        out_ref[h] = nn(hid_q, wc).astype(jnp.bfloat16)

    def update(h):
        @pl.when(b == 0)
        def _():
            wn[h] = init_ref[h]

        @pl.when(b > 0)
        def _():
            pass_copy(h).wait_recv()

        current = wn[h]
        grads = gsum[h, :, pl.ds(pl.multiple_of(z * rows, rows), rows), :]
        for d in range(1, outer):
            gz_arrival(h, d).wait_recv()
            grads = grads + gz[h, zid(d)].astype(jnp.float32)
        upd = current - grads
        ratio = jnp.sqrt(
            (jnp.mean(current * current, axis=-1, keepdims=True) + 1e-06)
            / (jnp.mean(upd * upd, axis=-1, keepdims=True) + 1e-06)
        )
        new_w = upd * ratio
        states_ref[h] = new_w
        sw[h] = new_w.astype(jnp.bfloat16)

        @pl.when(b < last)
        def _():
            for d in range(outer):
                next_copy(h, d).start()
            pass_copy(h).start()

    def guarded(fn, h, cond=None):
        ok = (h >= 0) & (h < heads)
        if cond is not None:
            ok = ok & cond

        @pl.when(ok)
        def _():
            fn(h)

    def step(i, _):
        guarded(start_init, i + AHEAD, b == 0)
        guarded(update, i - 2)
        guarded(combine, i - 1)
        guarded(differentiate, i + 0)
        guarded(forward_weights, i + 1)
        guarded(answer, i + 0)
        return 0

    lax.fori_loop(0, heads + DEPTH, step, 0)

    def drain(h, _):
        @pl.when(b == 0)
        def _():
            for d in range(1, outer):
                init_copy(h, d).wait_send()

        @pl.when(b < last)
        def _():
            for d in range(outer):
                next_copy(h, d).wait_send()
            pass_copy(h).wait_send()

        fwd_copy(h).wait_send()
        for m in range(3):
            gy_copy(h, m).wait_send()
        for d in range(1, outer):
            gz_copy(h, d).wait_send()
        return 0

    lax.fori_loop(0, heads, drain, 0)


def on_device(query, key, value, rates, init_weights):
    tokens, heads, dim = query.shape
    blocks, tok = lax.axis_size("block"), lax.axis_size("tok")
    outer = tok // PAIR
    rows, hid = init_weights.shape[2], init_weights.shape[2] * tok
    half = hid // PAIR
    factor = rates * (1.0 / math.sqrt(tokens * tok))
    g = (-(factor[:, :, None] * jnp.transpose(value, (1, 0, 2)).astype(jnp.float32))).astype(jnp.bfloat16)
    q = jnp.transpose(query, (1, 0, 2))
    k = jnp.transpose(key, (1, 0, 2))
    bf16, f32 = jnp.bfloat16, jnp.float32
    dma = pltpu.SemaphoreType.DMA
    vmem = pl.BlockSpec(memory_space=pltpu.VMEM)
    out, states = pl.pallas_call(
        functools.partial(kernel, heads, blocks, outer),
        out_shape=(
            jax.ShapeDtypeStruct((heads, tokens, dim), bf16),
            jax.ShapeDtypeStruct(init_weights.shape, f32),
        ),
        in_specs=[vmem] * 4,
        out_specs=(vmem, vmem),
        scratch_shapes=[
            pltpu.VMEM((heads, 3, hid, dim), bf16),
            pltpu.VMEM((heads, 3, rows, dim), bf16),
            pltpu.VMEM((heads, 3, rows, dim), bf16),
            pltpu.VMEM((heads, 3, rows, dim), f32),
            pltpu.VMEM((heads, 3, hid, dim), f32),
            pltpu.VMEM((heads, 3, half, dim), f32),
            pltpu.VMEM((heads, 3, half, dim), bf16),
            pltpu.VMEM((heads, 3, half, dim), bf16),
            pltpu.VMEM((heads, 3, half, dim), bf16),
            pltpu.VMEM((heads, outer, 3, rows, dim), bf16),
            dma((heads, outer)), dma((heads, outer)), dma((heads, outer)),
            dma((heads,)), dma((heads,)), dma((heads,)), dma((heads,)),
            dma((heads, 3)), dma((heads, 3)),
            dma((heads, outer)), dma((heads, outer)),
        ],
        compiler_params=pltpu.CompilerParams(
            collective_id=0, has_side_effects=True, vmem_limit_bytes=48 * 1024 * 1024
        ),
        cost_estimate=pl.CostEstimate(
            flops=18 * heads * tokens * hid * dim,
            bytes_accessed=10 * heads * tokens * dim,
            transcendentals=2 * heads * tokens * hid,
        ),
    )(q, k, g, init_weights)
    return (jnp.transpose(out, (1, 0, 2)), states[None])


def solution(mesh):
    placed = (
        P(("block", "tok"), None, None),
        P(("block", "tok"), None, None),
        P(("block", "tok"), None, None),
        P(None, ("block", "tok")),
        P(None, None, "tok", None),
    )
    return jax.shard_map(
        on_device,
        mesh=mesh,
        in_specs=placed,
        out_specs=(P(("block", "tok"), None, None), P("block", None, None, "tok", None)),
        check_vma=False,
    )
```

```python
import functools
import math

import jax
import jax.numpy as jnp
from jax import lax
from jax.experimental import pallas as pl
from jax.experimental.pallas import tpu as pltpu
from jax.sharding import PartitionSpec as P

MESH = pl.DeviceIdType.MESH
AHEAD = 1
PAIR = 2


def nt(left, right):
    return lax.dot_general(
        left, right, (((1,), (1,)), ((), ())), preferred_element_type=jnp.float32
    )


def nn(left, right):
    return lax.dot_general(
        left, right, (((1,), (0,)), ((), ())), preferred_element_type=jnp.float32
    )


def sigmoid(x):
    return 0.5 * jnp.tanh(0.5 * x) + 0.5


def kernel(
    heads, blocks, outer,
    q_ref, k_ref, g_ref, init_ref,
    out_ref, states_ref,
    wfull, wq, kp, gp, wn, nw, sw, iw, ip, sp, gf, sz, gz,
    kp_send, kp_recv, gp_send, gp_recv, ip_send, ip_recv, sp_send, sp_recv,
    wn_send, wn_recv, wq_send, wq_recv, wi_send, wz_send, wz_recv, gz_send, gz_recv,
):
    b = lax.axis_index("block")
    t = lax.axis_index("tok")
    z, y = t // PAIR, t % PAIR
    n = heads // PAIR
    rows = init_ref.shape[2]
    quarter = PAIR * rows
    my_rows = pl.ds(pl.multiple_of(y * rows, rows), rows)
    its_rows = pl.ds(pl.multiple_of((1 - y) * rows, rows), rows)
    last = blocks - 1
    late = b >= blocks // 2
    peer = (b, z * PAIR + (1 - y))
    following = lax.rem(b + 1, blocks)

    def zid(d):
        return lax.rem(z + d, outer)

    def part(d):
        return pl.ds(pl.multiple_of(zid(d) * quarter, quarter), quarter)

    def own(j):
        return y * n + j

    def other(j):
        return (1 - y) * n + j

    def copy(src, dst, send, recv, dev):
        return pltpu.make_async_remote_copy(
            src_ref=src, dst_ref=dst, send_sem=send, recv_sem=recv,
            device_id=dev, device_id_type=MESH,
        )

    def key_copy(j):
        return copy(k_ref.at[other(j)], kp.at[j], kp_send.at[j], kp_recv.at[j], peer)

    def g_copy(j):
        return copy(g_ref.at[other(j)], gp.at[j], gp_send.at[j], gp_recv.at[j], peer)

    def ip_copy(j):
        return copy(init_ref.at[other(j)], ip.at[j], ip_send.at[j], ip_recv.at[j], peer)

    def sp_copy(j):
        return copy(nw.at[j, :, its_rows, :], sp.at[j], sp_send.at[j], sp_recv.at[j], peer)

    def wq_copy(j):
        return copy(wfull.at[j], wq.at[j], wq_send.at[j], wq_recv.at[j], peer)

    def init_copy(j, d):
        return copy(iw.at[j], wfull.at[j, :, part(0), :], wi_send.at[j, d], wz_recv.at[j, z],
                    (b, zid(d) * PAIR + y))

    def next_copy(j, d):
        return copy(sw.at[j], wfull.at[j, :, part(0), :], wz_send.at[j, d], wz_recv.at[j, z],
                    (following, zid(d) * PAIR + y))

    def wz_arrival(j, d):
        return copy(sw.at[j], wfull.at[j, :, part(d), :], wz_send.at[j, d],
                    wz_recv.at[j, zid(d)], peer)

    def pass_copy(j):
        return copy(nw.at[j], wn.at[j], wn_send.at[j], wn_recv.at[j], (following, t))

    def gz_copy(j, d):
        return copy(sz.at[j, :, part(d), :], gz.at[j, z], gz_send.at[j, d], gz_recv.at[j, z],
                    (b, zid(d) * PAIR + y))

    def gz_arrival(j, d):
        return copy(sz.at[j, :, part(d), :], gz.at[j, zid(d)], gz_send.at[j, d],
                    gz_recv.at[j, zid(d)], peer)

    barrier = pltpu.get_barrier_semaphore()

    def greet(dev):
        pl.semaphore_signal(barrier, inc=1, device_id=dev, device_id_type=MESH)

    greet(peer)
    for d in range(1, outer):
        greet((b, zid(d) * PAIR + y))
    for d in range(outer):
        greet((following, zid(d) * PAIR + y))
        greet((lax.rem(b + last, blocks), zid(d) * PAIR + y))
    pl.semaphore_wait(barrier, 3 * outer)

    def start_tokens(j):
        @pl.when(b == 0)
        def _():
            ip_copy(j).start()

        key_copy(j).start()
        g_copy(j).start()

    def start_init(j):
        ip_copy(j).wait_recv()
        wn[j, :, my_rows, :] = init_ref[own(j)]
        wn[j, :, its_rows, :] = ip[j]
        iw[j] = wn[j].astype(jnp.bfloat16)
        wfull[j, :, part(0), :] = iw[j]
        for d in range(1, outer):
            init_copy(j, d).start()

    for j in range(min(AHEAD, n)):
        start_tokens(j)

    @pl.when(late)
    def _():
        for j in range(min(AHEAD, n), n):
            start_tokens(j)

    @pl.when(b == 0)
    def _():
        for j in range(min(AHEAD, n)):
            start_init(j)

    def differentiate(j):
        for d in range(1, outer):
            wz_arrival(j, d).wait_recv()

        @pl.when(b > 0)
        def _():
            wz_arrival(j, 0).wait_recv()

        key_copy(j).wait_recv()
        g_copy(j).wait_recv()
        wa, wb, wc = wfull[j, 0], wfull[j, 1], wfull[j, 2]

        def terms(keys, g):
            a = nt(wa, keys)
            bb = nt(wb, keys)
            sig = sigmoid(a)
            s = a * sig
            hid = (s * bb).astype(jnp.bfloat16)
            dhid = nt(wc, g)
            db = (dhid * s).astype(jnp.bfloat16)
            da = (dhid * bb * (sig * (1.0 + a * (1.0 - sig)))).astype(jnp.bfloat16)
            return nn(da, keys), nn(db, keys), nn(hid, g)

        for m, grad in enumerate(terms(k_ref[own(j)], g_ref[own(j)])):
            gf[j, m] = grad
        for m, grad in enumerate(terms(kp[j], gp[j])):
            total = gf[j, m] + grad
            gf[j, m] = total
            sz[j, m] = total.astype(jnp.bfloat16)
        for d in range(1, outer):
            gz_copy(j, d).start()

    def lend(j):
        wq_copy(j).start()

    def respond(h, weights, j):
        quer = q_ref[h]
        qa = nt(quer, weights[j, 0])
        hid_q = (qa * sigmoid(qa) * nt(quer, weights[j, 1])).astype(jnp.bfloat16)
        out_ref[h] = nn(hid_q, weights[j, 2]).astype(jnp.bfloat16)

    def answer(j):
        respond(own(j), wfull, j)

    def answer_other(j):
        wq_copy(j).wait_recv()
        respond(other(j), wq, j)

    def update(j):
        @pl.when(b > 0)
        def _():
            pass_copy(j).wait_recv()

        current = wn[j]
        grads = gf[j, :, part(0), :]
        for d in range(1, outer):
            gz_arrival(j, d).wait_recv()
            grads = grads + gz[j, zid(d)].astype(jnp.float32)
        upd = current - grads
        ratio = jnp.sqrt(
            (jnp.mean(current * current, axis=-1, keepdims=True) + 1e-06)
            / (jnp.mean(upd * upd, axis=-1, keepdims=True) + 1e-06)
        )
        new_w = upd * ratio
        nw[j] = new_w
        sw[j] = new_w.astype(jnp.bfloat16)

        @pl.when(b < last)
        def _():
            for d in range(outer):
                next_copy(j, d).start()
            pass_copy(j).start()

        sp_copy(j).start()
        states_ref[own(j)] = nw[j, :, my_rows, :]

    def guarded(fn, j, cond=None):
        ok = (j >= 0) & (j < n)
        if cond is not None:
            ok = ok & cond

        @pl.when(ok)
        def _():
            fn(j)

    def step(i, _):
        guarded(differentiate, i)
        guarded(start_tokens, i + AHEAD, jnp.logical_not(late))
        guarded(start_init, i + AHEAD, b == 0)
        guarded(lend, i, late)
        guarded(answer, i)
        guarded(answer_other, i - 1, late)
        guarded(update, i)
        return 0

    lax.fori_loop(0, n + 1, step, 0)

    def finish(j, _):
        lend(j)
        return 0

    def finish_other(j, _):
        answer_other(j)
        return 0

    @pl.when(jnp.logical_not(late))
    def _():
        lax.fori_loop(0, n, finish, 0)
        lax.fori_loop(0, n, finish_other, 0)

    def drain(j, _):
        sp_copy(j).wait_recv()
        states_ref[other(j)] = sp[j]

        @pl.when(b == 0)
        def _():
            ip_copy(j).wait_send()
            for d in range(1, outer):
                init_copy(j, d).wait_send()

        @pl.when(b < last)
        def _():
            for d in range(outer):
                next_copy(j, d).wait_send()
            pass_copy(j).wait_send()

        key_copy(j).wait_send()
        g_copy(j).wait_send()
        sp_copy(j).wait_send()
        wq_copy(j).wait_send()
        for d in range(1, outer):
            gz_copy(j, d).wait_send()
        return 0

    lax.fori_loop(0, n, drain, 0)


def on_device(query, key, value, rates, init_weights):
    tokens, heads, dim = query.shape
    blocks, tok = lax.axis_size("block"), lax.axis_size("tok")
    outer = tok // PAIR
    rows, hid = init_weights.shape[2], init_weights.shape[2] * tok
    quarter, n = PAIR * rows, heads // PAIR
    factor = rates * (1.0 / math.sqrt(tokens * tok))
    g = (-(factor[:, :, None] * jnp.transpose(value, (1, 0, 2)).astype(jnp.float32))).astype(jnp.bfloat16)
    q = jnp.transpose(query, (1, 0, 2))
    k = jnp.transpose(key, (1, 0, 2))
    bf16, f32 = jnp.bfloat16, jnp.float32
    dma = pltpu.SemaphoreType.DMA
    vmem = pl.BlockSpec(memory_space=pltpu.VMEM)
    out, states = pl.pallas_call(
        functools.partial(kernel, heads, blocks, outer),
        out_shape=(
            jax.ShapeDtypeStruct((heads, tokens, dim), bf16),
            jax.ShapeDtypeStruct(init_weights.shape, f32),
        ),
        in_specs=[vmem] * 4,
        out_specs=(vmem, vmem),
        scratch_shapes=[
            pltpu.VMEM((n, 3, hid, dim), bf16),
            pltpu.VMEM((n, 3, hid, dim), bf16),
            pltpu.VMEM((n, tokens, dim), bf16),
            pltpu.VMEM((n, tokens, dim), bf16),
            pltpu.VMEM((n, 3, quarter, dim), f32),
            pltpu.VMEM((n, 3, quarter, dim), f32),
            pltpu.VMEM((n, 3, quarter, dim), bf16),
            pltpu.VMEM((n, 3, quarter, dim), bf16),
            pltpu.VMEM((n, 3, rows, dim), f32),
            pltpu.VMEM((n, 3, rows, dim), f32),
            pltpu.VMEM((n, 3, hid, dim), f32),
            pltpu.VMEM((n, 3, hid, dim), bf16),
            pltpu.VMEM((n, outer, 3, quarter, dim), bf16),
        ] + [dma((n,))] * 12 + [dma((n, outer))] * 5,
        compiler_params=pltpu.CompilerParams(
            collective_id=0, has_side_effects=True, vmem_limit_bytes=48 * 1024 * 1024
        ),
        cost_estimate=pl.CostEstimate(
            flops=18 * heads * tokens * hid * dim,
            bytes_accessed=10 * heads * tokens * dim,
            transcendentals=2 * heads * tokens * hid,
        ),
    )(q, k, g, init_weights)
    return (jnp.transpose(out, (1, 0, 2)), states[None])


def solution(mesh):
    placed = (
        P(("block", "tok"), None, None),
        P(("block", "tok"), None, None),
        P(("block", "tok"), None, None),
        P(None, ("block", "tok")),
        P(None, None, "tok", None),
    )
    return jax.shard_map(
        on_device,
        mesh=mesh,
        in_specs=placed,
        out_specs=(P(("block", "tok"), None, None), P("block", None, None, "tok", None)),
        check_vma=False,
    )
```
